32 devices in a mesh: groups: 2 (over x), res: 16 (over z, y, core).
Axes of the slice: x: 2, y: 2, z: 4, core: 2. Of those that a mesh axis runs over, the one named last changes fastest.
Arguments:
- pair_left: bfloat16 [2048, 64, 128], P(('groups', 'res')), parts along dimension 0, may hold values from -6 to 6
- pair_right: bfloat16 [2048, 256, 128], P(('groups', 'res')), parts along dimension 0, may hold values from -6 to 6
- pair_block: bfloat16 [512, 64, 128], P(('groups', 'res')), parts along dimension 0, may hold values from -6 to 6
- grad_out: bfloat16 [512, 64, 128], P(('groups', 'res')), parts along dimension 0, may hold values from -6 to 6
- norm_gain: float32 [128], replicated, may hold values from 0.25 to 1.75
- norm_bias: float32 [128], replicated, may hold values from -3 to 3
- weight_left: bfloat16 [128, 128], replicated, may hold values from -0.5 to 0.5
- gate_left: bfloat16 [128, 128], replicated, may hold values from -0.5 to 0.5
- weight_right: bfloat16 [128, 128], replicated, may hold values from -0.5 to 0.5
- gate_right: bfloat16 [128, 128], replicated, may hold values from -0.5 to 0.5
- tri_gain: float32 [128], replicated, may hold values from 0.25 to 1.75
- tri_bias: float32 [128], replicated, may hold values from -3 to 3
- weight_out: bfloat16 [128, 128], replicated, may hold values from -0.5 to 0.5
- gate_out: bfloat16 [128, 128], replicated, may hold values from -0.5 to 0.5
- tile_left: int32 [32, 4], P(('groups', 'res')), parts along dimension 0, may hold values 0 or 1
- tile_right: int32 [32, 16], P(('groups', 'res')), parts along dimension 0, may hold values 0 or 1
- chain_rows: int32 [2048], P(('groups', 'res')), parts along dimension 0, may hold values from 0 to 5, never falling along the last dimension, each value on 1 to 256 neighbouring positions
- chain_slab: int32 [128], P('groups'), parts along dimension 0, may hold values from 0 to 5, never falling along the last dimension, each value on 1 to 16 neighbouring positions
- chain_cols: int32 [512], P('groups'), parts along dimension 0, may hold values from 0 to 5, never falling along the last dimension, each value on 1 to 64 neighbouring positions
Outputs:
- grad_left: bfloat16 [2048, 64, 128], P(('groups', 'res')), parts along dimension 0
- grad_right: bfloat16 [2048, 256, 128], P(('groups', 'res')), parts along dimension 0
- grad_block: bfloat16 [512, 64, 128], P(('groups', 'res')), parts along dimension 0
The draws below stay inside these ranges and needn't reach their ends.
There are 2 independent parts, one for each index of `groups`. The reference program is written for one: setup_inputs(seed, part) draws one part's arguments, and reference() takes and returns one part's arrays. A program takes and returns all parts, laid end to end along the dimension named above; an argument that names none is the same for every part. Nothing has to cross between parts.
All inputs are finite; a program needn't handle non-finite values. No bound on the sum of `tile_left` or of `tile_right` on one device may be relied on, other than what follows from the above.
Results may differ from the reference program's by a relative error of at most 0.017.
Values may be sent and summed in bfloat16 or wider, within the bound.
A program may use at most 320 MiB of HBM per device.

```python
import math
import jax
import jax.numpy as jnp
import numpy as np
from jax import lax

CZ = 128
CH = 128
KR_DEV = 64
J_DEV = 16
SLAB = 64
ITILES = 4
K = 1024
J = 256
N_RES = 16


def touch_ends(values, stream_key, least, top_value):
    place = [jax.random.randint(jax.random.fold_in(stream_key, axis), (), 0, length) for axis, length in enumerate(values.shape)]
    longest = values.shape.index(max(values.shape))
    neighbour = place[:longest] + [(place[longest] + 1) % values.shape[longest]] + place[longest + 1:]
    return values.at[tuple(place)].set(least).at[tuple(neighbour)].set(top_value)


def levels(own_key, shape, cuts, low, high):
    level = 1.0
    for dim, blocks in cuts:
        draws = jax.random.uniform(jax.random.fold_in(jax.random.fold_in(own_key, 6), dim), (blocks,), jnp.float32, low / len(cuts), high / len(cuts))
        level = level * jnp.repeat(jnp.exp(draws), shape[dim] // blocks).reshape((-1,) + (1,) * (len(shape) - 1 - dim))
    return level


def length_profile(count, total, limit, slope):
    weights = [(1 << 20) // math.isqrt(standing ** slope) + 1 for standing in range(2, count + 1)]
    surplus, counts = total - limit - (count - 1), [1] * (count - 1)
    while surplus > 0:
        free = [i for i in range(count - 1) if counts[i] < limit]
        mass, left = sum([weights[i] for i in free]), surplus
        for i in free:
            more = min(limit - counts[i], max(1, left * weights[i] // mass), surplus)
            counts[i] = counts[i] + more
            surplus = surplus - more
    return np.array([limit] + counts)


def ragged(own_key, amount, total, bound, lean):
    if amount == 2:
        one = jax.random.randint(own_key, (), max(1, total - bound), min(bound, total - 1) + 1)
        return jnp.stack([one, total - one])
    sizes = jnp.asarray(length_profile(amount, total, bound, lean), jnp.int32)
    twos = (amount - 1) // 2
    source_of, sink = sizes[1:1 + 2 * twos:2], sizes[2:2 + 2 * twos:2]
    slack = jnp.minimum(source_of - 1, bound - sink)
    moved = jax.random.randint(jax.random.fold_in(own_key, 1), (twos,), 0, 1 << 20) % (slack + 1)
    sizes = sizes.at[1:1 + 2 * twos:2].set(source_of - moved).at[2:2 + 2 * twos:2].set(sink + moved)
    return sizes[jax.random.permutation(jax.random.fold_in(own_key, 2), amount)]


def normal_values(own_key, dims, scale, limit, split=(), dtype=jnp.bfloat16):
    array = scale * jax.random.normal(own_key, dims, jnp.float32)
    if split:
        array = array * levels(own_key, dims, split, -0.22, 0.18)
    return jnp.clip(array, -limit, limit).astype(dtype)


def setup_inputs(seed: int = 0, part: int = 0) -> dict:
    key_of = jax.random.split(jax.random.key(seed), 20)
    own_keys = jax.random.split(jax.random.fold_in(key_of[19], part), 20)
    pair_left = normal_values(own_keys[0], (K, SLAB, CZ), 1.0, 6.0, ((0, 16),))
    pair_right = normal_values(own_keys[1], (K, J, CZ), 1.0, 6.0, ((0, 16),))
    pair_block = normal_values(own_keys[2], (J, SLAB, CZ), 1.0, 6.0, ((0, 16),))
    grad_out = normal_values(own_keys[3], (J, SLAB, CZ), 1.0, 6.0, ((0, 16),))
    norm_gain = jnp.clip(1.0 + 0.15 * jax.random.normal(key_of[4], (CZ,), jnp.float32), 0.25, 1.75)
    norm_bias = normal_values(key_of[5], (CZ,), 0.5, 3.0, (), jnp.float32)
    weight_left = normal_values(key_of[6], (CZ, CH), CZ ** -0.5, 0.5)
    gate_left = normal_values(key_of[7], (CZ, CH), CZ ** -0.5, 0.5)
    weight_right = normal_values(key_of[8], (CZ, CH), CZ ** -0.5, 0.5)
    gate_right = normal_values(key_of[9], (CZ, CH), CZ ** -0.5, 0.5)
    tri_gain = jnp.clip(1.0 + 0.15 * jax.random.normal(key_of[10], (CH,), jnp.float32), 0.25, 1.75)
    tri_bias = normal_values(key_of[11], (CH,), 0.5, 3.0, (), jnp.float32)
    weight_out = normal_values(key_of[12], (CH, CZ), CH ** -0.5, 0.5)
    gate_out = normal_values(key_of[13], (CZ, CZ), CZ ** -0.5, 0.5)
    tile_left = touch_ends((jax.random.randint(own_keys[14], (N_RES, ITILES), 0, 4) < 1).astype(jnp.int32), jax.random.fold_in(own_keys[14], 1), 0, 1)
    tile_right = touch_ends((jax.random.randint(own_keys[15], (N_RES, N_RES), 0, 4) < 1).astype(jnp.int32), jax.random.fold_in(own_keys[15], 1), 0, 1)
    chain_rows = jnp.searchsorted(jnp.cumsum(ragged(own_keys[16], 6, K, K // 4, 2)), jnp.arange(K), side="right").astype(jnp.int32)
    chain_slab = jnp.searchsorted(jnp.cumsum(ragged(own_keys[17], 6, SLAB, SLAB // 4, 2)), jnp.arange(SLAB), side="right").astype(jnp.int32)
    chain_cols = jnp.searchsorted(jnp.cumsum(ragged(own_keys[18], 6, J, J // 4, 2)), jnp.arange(J), side="right").astype(jnp.int32)
    return {"pair_left": pair_left, "pair_right": pair_right, "pair_block": pair_block, "grad_out": grad_out, "norm_gain": norm_gain, "norm_bias": norm_bias, "weight_left": weight_left, "gate_left": gate_left, "weight_right": weight_right, "gate_right": gate_right, "tri_gain": tri_gain, "tri_bias": tri_bias, "weight_out": weight_out, "gate_out": gate_out, "tile_left": tile_left, "tile_right": tile_right, "chain_rows": chain_rows, "chain_slab": chain_slab, "chain_cols": chain_cols}


def layer_norm(values, gain, bias):
    values = values.astype(jnp.float32)
    center = lax.optimization_barrier(jnp.mean(values, axis=-1, keepdims=True))
    spread = lax.optimization_barrier(jnp.mean(jnp.square(values - center), axis=-1, keepdims=True))
    return (values - center) * lax.rsqrt(spread + 1e-05) * gain + bias

def projection(pair, mask, norm_gain, norm_bias, weight, gate):
    normed = layer_norm(pair, norm_gain, norm_bias).astype(jnp.bfloat16)
    value = jnp.dot(normed, weight, preferred_element_type=jnp.float32)
    gating = jax.nn.sigmoid(jnp.dot(normed, gate, preferred_element_type=jnp.float32))
    return mask[..., None] * gating * value

def output_gate(tri, pair, norm_gain, norm_bias, tri_gain, tri_bias, weight_out, gate_out):
    normed = layer_norm(pair, norm_gain, norm_bias).astype(jnp.bfloat16)
    gating = jax.nn.sigmoid(jnp.dot(normed, gate_out, preferred_element_type=jnp.float32))
    scaled = layer_norm(tri, tri_gain, tri_bias).astype(jnp.bfloat16)
    return gating * jnp.dot(scaled, weight_out, preferred_element_type=jnp.float32)

def reference(pair_left, pair_right, pair_block, grad_out, norm_gain, norm_bias, weight_left, gate_left, weight_right, gate_right, tri_gain, tri_bias, weight_out, gate_out, tile_left, tile_right, chain_rows, chain_slab, chain_cols):
    same_left = (chain_rows[:, None] == chain_slab[None, :]).astype(jnp.int32)
    mask_left = jnp.maximum(jnp.repeat(jnp.repeat(tile_left, KR_DEV, axis=0), SLAB // ITILES, axis=1), same_left).astype(jnp.float32)
    same_right = (chain_rows[:, None] == chain_cols[None, :]).astype(jnp.int32)
    mask_right = jnp.maximum(jnp.repeat(jnp.repeat(tile_right, KR_DEV, axis=0), J_DEV, axis=1), same_right).astype(jnp.float32)
    left_full, left_back = jax.vjp(lambda pair: projection(pair, mask_left, norm_gain, norm_bias, weight_left, gate_left), pair_left)
    right_full, right_back = jax.vjp(lambda pair: projection(pair, mask_right, norm_gain, norm_bias, weight_right, gate_right), pair_right)
    left = left_full.astype(jnp.bfloat16)
    right = right_full.astype(jnp.bfloat16)
    tri = jnp.einsum('kic,kjc->jic', left.astype(jnp.float32), right.astype(jnp.float32))
    result, out_back = jax.vjp(lambda product, pair: output_gate(product, pair, norm_gain, norm_bias, tri_gain, tri_bias, weight_out, gate_out), tri, pair_block)
    grad_tri, block_grad = out_back(grad_out.astype(jnp.float32))
    sent = grad_tri.astype(jnp.bfloat16)
    grad_proj_left = jnp.einsum('jic,kjc->kic', sent.astype(jnp.float32), right.astype(jnp.float32))
    grad_proj_right = jnp.einsum('kic,jic->kjc', left.astype(jnp.float32), sent.astype(jnp.float32))
    grad_left, = left_back(grad_proj_left)
    grad_right, = right_back(grad_proj_right)
    return (grad_left.astype(jnp.bfloat16), grad_right.astype(jnp.bfloat16), block_grad.astype(jnp.bfloat16))
```

```python
import jax
import jax.numpy as jnp
from jax import lax
from jax.sharding import PartitionSpec as P


def layer_norm(values, gain, bias):
    values = values.astype(jnp.float32)
    center = jnp.mean(values, axis=-1, keepdims=True)
    spread = jnp.mean(jnp.square(values - center), axis=-1, keepdims=True)
    return (values - center) * lax.rsqrt(spread + 1e-05) * gain + bias


def projection(pair, mask, norm_gain, norm_bias, weight, gate):
    normed = layer_norm(pair, norm_gain, norm_bias).astype(jnp.bfloat16)
    value = jnp.dot(normed, weight, preferred_element_type=jnp.float32)
    gating = jax.nn.sigmoid(jnp.dot(normed, gate, preferred_element_type=jnp.float32))
    return mask[..., None] * gating * value


def output_gate(tri, pair, norm_gain, norm_bias, tri_gain, tri_bias, weight_out, gate_out):
    normed = layer_norm(pair, norm_gain, norm_bias).astype(jnp.bfloat16)
    gating = jax.nn.sigmoid(jnp.dot(normed, gate_out, preferred_element_type=jnp.float32))
    scaled = layer_norm(tri, tri_gain, tri_bias).astype(jnp.bfloat16)
    return gating * jnp.dot(scaled, weight_out, preferred_element_type=jnp.float32)


def local(
    pair_left,
    pair_right,
    pair_block,
    grad_out,
    norm_gain,
    norm_bias,
    weight_left,
    gate_left,
    weight_right,
    gate_right,
    tri_gain,
    tri_bias,
    weight_out,
    gate_out,
    tile_left,
    tile_right,
    chain_rows,
    chain_slab,
    chain_cols,
):
    slab_rows = pair_left.shape[1]
    block_cols = pair_block.shape[0]
    tile_rows = slab_rows // tile_left.shape[1]
    same_left = (chain_rows[:, None] == chain_slab[None, :]).astype(jnp.int32)
    mask_left = jnp.maximum(jnp.repeat(tile_left, tile_rows, axis=1), same_left).astype(jnp.float32)
    same_right = (chain_rows[:, None] == chain_cols[None, :]).astype(jnp.int32)
    mask_right = jnp.maximum(jnp.repeat(tile_right, block_cols, axis=1), same_right).astype(
        jnp.float32
    )
    left_full, left_back = jax.vjp(
        lambda pair: projection(pair, mask_left, norm_gain, norm_bias, weight_left, gate_left),
        pair_left,
    )
    right_full, right_back = jax.vjp(
        lambda pair: projection(pair, mask_right, norm_gain, norm_bias, weight_right, gate_right),
        pair_right,
    )
    left = left_full.astype(jnp.bfloat16)
    right = right_full.astype(jnp.bfloat16)
    tri = lax.psum_scatter(
        jnp.einsum("kic,kjc->jic", left, right, preferred_element_type=jnp.float32).astype(jnp.bfloat16),
        "res",
        scatter_dimension=0,
        tiled=True,
    ).astype(jnp.float32)
    result, out_back = jax.vjp(
        lambda product, pair: output_gate(
            product, pair, norm_gain, norm_bias, tri_gain, tri_bias, weight_out, gate_out
        ),
        tri,
        pair_block,
    )
    grad_tri, block_grad = out_back(grad_out.astype(jnp.float32))
    sent = grad_tri.astype(jnp.bfloat16)

    gathered = lax.all_gather(sent, "res", axis=0, tiled=True)
    total_left = jnp.einsum("jic,kjc->kic", gathered, right, preferred_element_type=jnp.float32)
    total_right = jnp.einsum("kic,jic->kjc", left, gathered, preferred_element_type=jnp.float32)
    (grad_left,) = left_back(total_left)
    (grad_right,) = right_back(total_right)
    return (grad_left, grad_right, block_grad)


def solution(mesh):
    placed = (
        P(("groups", "res"), None, None),
        P(("groups", "res"), None, None),
        P(("groups", "res"), None, None),
        P(("groups", "res"), None, None),
        P(),
        P(),
        P(),
        P(),
        P(),
        P(),
        P(),
        P(),
        P(),
        P(),
        P(("groups", "res"), None),
        P(("groups", "res"), None),
        P(("groups", "res")),
        P("groups"),
        P("groups"),
    )
    return jax.shard_map(
        local,
        mesh=mesh,
        in_specs=placed,
        out_specs=(
            P(("groups", "res"), None, None),
            P(("groups", "res"), None, None),
            P(("groups", "res"), None, None),
        ),
        check_vma=False,
    )
```

```python
import functools

import jax
import jax.numpy as jnp
from jax import lax
from jax.experimental import pallas as pl
from jax.experimental.pallas import tpu as pltpu
from jax.sharding import PartitionSpec as P


MESH = pl.DeviceIdType.MESH
VMEM_LIMIT = 48 * 1024 * 1024


def bits_of(count):
    return count.bit_length() - 1


def peer(me, rel):
    other = me
    for s in range(rel.bit_length()):
        if (rel >> s) & 1:
            step = 1 << s
            other = other + step * (1 - 2 * lax.rem(lax.div(me, step), 2))
    return other


def greet(me, stages):
    barrier = pltpu.get_barrier_semaphore()
    for s in range(stages):
        pl.semaphore_signal(
            barrier, inc=1, device_id={"res": peer(me, 1 << s)}, device_id_type=MESH
        )
    pl.semaphore_wait(barrier, stages)


def scatter_kernel(n, x_ref, out_ref, acc, recv, send_sem, recv_sem):
    me = lax.axis_index("res")
    stages = bits_of(n)
    greet(me, stages)
    base = [n - (n >> s) for s in range(stages)]

    def copy(s, h):
        rel = (2 * h + 1) << s
        slot = base[s] + h
        return pltpu.make_async_remote_copy(
            src_ref=x_ref.at[peer(me, rel)] if s == 0 else acc.at[rel // 2],
            dst_ref=recv.at[slot],
            send_sem=send_sem.at[slot],
            recv_sem=recv_sem.at[slot],
            device_id={"res": peer(me, 1 << s)},
            device_id_type=MESH,
        )

    def order(s):
        names = range(n >> (s + 1))
        return sorted(names, key=lambda h: ((h & -h) or n, -h))

    copies = {}
    for h in order(0):
        copies[0, h] = copy(0, h)
        copies[0, h].start()
    rows = x_ref.shape[1]
    part = min(rows, 128)
    for s in range(stages):
        for h in order(s):
            copies[s, h].wait_recv()
            rel = h << (s + 1)
            slot = base[s] + h
            source = x_ref.at[peer(me, rel)] if s == 0 else acc.at[rel // 2]

            @pl.loop(0, rows // part)
            def _(r):
                at = pl.ds(pl.multiple_of(r * part, part), part)
                total = source[at].astype(jnp.float32) + recv[slot, at].astype(jnp.float32)
                if s == stages - 1:
                    out_ref[at] = total
                else:
                    acc[rel // 2, at] = total.astype(jnp.bfloat16)

            if h % 2 == 1:
                copies[s + 1, h // 2] = copy(s + 1, h // 2)
                copies[s + 1, h // 2].start()
    for each in copies.values():
        each.wait_send()


def reduce_scatter(blocks):
    n, rows, width = blocks.shape
    return pl.pallas_call(
        functools.partial(scatter_kernel, n),
        out_shape=jax.ShapeDtypeStruct((rows, width), jnp.float32),
        in_specs=[pl.BlockSpec(memory_space=pltpu.VMEM)],
        out_specs=pl.BlockSpec(memory_space=pltpu.VMEM),
        scratch_shapes=[
            pltpu.VMEM((n // 2, rows, width), jnp.bfloat16),
            pltpu.VMEM((n - 1, rows, width), jnp.bfloat16),
            pltpu.SemaphoreType.DMA((n - 1,)),
            pltpu.SemaphoreType.DMA((n - 1,)),
        ],
        compiler_params=pltpu.CompilerParams(
            collective_id=0, has_side_effects=True, vmem_limit_bytes=VMEM_LIMIT
        ),
        name="reduce_scatter",
    )(blocks)


def gather_kernel(n, x_ref, out_ref, send_sem, recv_sem):
    me = lax.axis_index("res")
    stages = bits_of(n)
    greet(me, stages)
    base = [n - (n >> s) for s in range(stages)]

    def copy(s, h):
        owner = peer(me, h << (s + 1))
        slot = base[s] + h
        return pltpu.make_async_remote_copy(
            src_ref=x_ref if h == 0 else out_ref.at[owner],
            dst_ref=out_ref.at[owner],
            send_sem=send_sem.at[slot],
            recv_sem=recv_sem.at[slot],
            device_id={"res": peer(me, 1 << s)},
            device_id_type=MESH,
        )

    copies = {}

    def pass_on(rel, stage):
        for s in reversed(range(stage)):
            copies[s, rel >> (s + 1)] = copy(s, rel >> (s + 1))
            copies[s, rel >> (s + 1)].start()

    pass_on(0, stages)
    out_ref[me] = x_ref[...]
    waits = [(s, h) for s in range(stages) for h in range(n >> (s + 1))]
    hops = lambda s, h: bin((2 * h + 1) << s).count("1")
    waits.sort(key=lambda sh: (hops(*sh) - stages, sh) if sh[0] >= 2 else (stages - sh[0], sh))
    for s, h in waits:
        copies[s, h].wait_recv()
        pass_on((2 * h + 1) << s, s)
    for each in copies.values():
        each.wait_send()


def all_gather(block, n):
    rows, width = block.shape
    return pl.pallas_call(
        functools.partial(gather_kernel, n),
        out_shape=jax.ShapeDtypeStruct((n, rows, width), block.dtype),
        in_specs=[pl.BlockSpec(memory_space=pltpu.VMEM)],
        out_specs=pl.BlockSpec(memory_space=pltpu.VMEM),
        scratch_shapes=[
            pltpu.SemaphoreType.DMA((n - 1,)),
            pltpu.SemaphoreType.DMA((n - 1,)),
        ],
        compiler_params=pltpu.CompilerParams(
            collective_id=1, has_side_effects=True, vmem_limit_bytes=VMEM_LIMIT
        ),
        name="all_gather",
    )(block)


def layer_norm(values, gain, bias):
    values = values.astype(jnp.float32)
    center = jnp.mean(values, axis=-1, keepdims=True)
    spread = jnp.mean(jnp.square(values - center), axis=-1, keepdims=True)
    return (values - center) * lax.rsqrt(spread + 1e-05) * gain + bias


def projection(pair, mask, norm_gain, norm_bias, weight, gate):
    normed = layer_norm(pair, norm_gain, norm_bias).astype(jnp.bfloat16)
    value = jnp.dot(normed, weight, preferred_element_type=jnp.float32)
    gating = jax.nn.sigmoid(jnp.dot(normed, gate, preferred_element_type=jnp.float32))
    return mask[..., None] * gating * value


def output_gate(tri, pair, norm_gain, norm_bias, tri_gain, tri_bias, weight_out, gate_out):
    normed = layer_norm(pair, norm_gain, norm_bias).astype(jnp.bfloat16)
    gating = jax.nn.sigmoid(jnp.dot(normed, gate_out, preferred_element_type=jnp.float32))
    scaled = layer_norm(tri, tri_gain, tri_bias).astype(jnp.bfloat16)
    return gating * jnp.dot(scaled, weight_out, preferred_element_type=jnp.float32)


def local(
    pair_left,
    pair_right,
    pair_block,
    grad_out,
    norm_gain,
    norm_bias,
    weight_left,
    gate_left,
    weight_right,
    gate_right,
    tri_gain,
    tri_bias,
    weight_out,
    gate_out,
    tile_left,
    tile_right,
    chain_rows,
    chain_slab,
    chain_cols,
):
    slab_rows = pair_left.shape[1]
    block_cols = pair_block.shape[0]
    tile_rows = slab_rows // tile_left.shape[1]
    same_left = (chain_rows[:, None] == chain_slab[None, :]).astype(jnp.int32)
    mask_left = jnp.maximum(jnp.repeat(tile_left, tile_rows, axis=1), same_left).astype(jnp.float32)
    same_right = (chain_rows[:, None] == chain_cols[None, :]).astype(jnp.int32)
    mask_right = jnp.maximum(jnp.repeat(tile_right, block_cols, axis=1), same_right).astype(
        jnp.float32
    )
    left_full, left_back = jax.vjp(
        lambda pair: projection(pair, mask_left, norm_gain, norm_bias, weight_left, gate_left),
        pair_left,
    )
    right_full, right_back = jax.vjp(
        lambda pair: projection(pair, mask_right, norm_gain, norm_bias, weight_right, gate_right),
        pair_right,
    )
    left = left_full.astype(jnp.bfloat16)
    right = right_full.astype(jnp.bfloat16)
    col_total, hidden = right.shape[1:]
    axis_size = col_total // block_cols
    share = jnp.einsum("kic,kjc->jic", left, right, preferred_element_type=jnp.float32)
    tri = reduce_scatter(
        share.astype(jnp.bfloat16).reshape(axis_size, block_cols * slab_rows, hidden)
    ).reshape(block_cols, slab_rows, hidden)
    result, out_back = jax.vjp(
        lambda product, pair: output_gate(
            product, pair, norm_gain, norm_bias, tri_gain, tri_bias, weight_out, gate_out
        ),
        tri,
        pair_block,
    )
    grad_tri, block_grad = out_back(grad_out.astype(jnp.float32))
    sent = grad_tri.astype(jnp.bfloat16)

    gathered = all_gather(sent.reshape(block_cols * slab_rows, hidden), axis_size)
    gathered = gathered.reshape(col_total, slab_rows, hidden)
    total_left = jnp.einsum("jic,kjc->kic", gathered, right, preferred_element_type=jnp.float32)
    total_right = jnp.einsum("kic,jic->kjc", left, gathered, preferred_element_type=jnp.float32)
    (grad_left,) = left_back(total_left)
    (grad_right,) = right_back(total_right)
    return (grad_left, grad_right, block_grad)


def solution(mesh):
    placed = (
        P(("groups", "res"), None, None),
        P(("groups", "res"), None, None),
        P(("groups", "res"), None, None),
        P(("groups", "res"), None, None),
        P(),
        P(),
        P(),
        P(),
        P(),
        P(),
        P(),
        P(),
        P(),
        P(),
        P(("groups", "res"), None),
        P(("groups", "res"), None),
        P(("groups", "res")),
        P("groups"),
        P("groups"),
    )
    return jax.shard_map(
        local,
        mesh=mesh,
        in_specs=placed,
        out_specs=(
            P(("groups", "res"), None, None),
            P(("groups", "res"), None, None),
            P(("groups", "res"), None, None),
        ),
        check_vma=False,
    )
```

```python
import functools

import jax
import jax.numpy as jnp
from jax import lax
from jax.experimental import pallas as pl
from jax.experimental.pallas import tpu as pltpu
from jax.sharding import PartitionSpec as P


MESH = pl.DeviceIdType.MESH
VMEM_LIMIT = 48 * 1024 * 1024


def bits_of(count):
    return count.bit_length() - 1


def peer(me, rel):
    other = me
    for s in range(rel.bit_length()):
        if (rel >> s) & 1:
            step = 1 << s
            other = other + step * (1 - 2 * lax.rem(lax.div(me, step), 2))
    return other


def greet(me, stages):
    barrier = pltpu.get_barrier_semaphore()
    for s in range(stages):
        pl.semaphore_signal(
            barrier, inc=1, device_id={"res": peer(me, 1 << s)}, device_id_type=MESH
        )
    pl.semaphore_wait(barrier, stages)


def scatter_kernel(n, x_ref, out_ref, acc, recv, send_sem, recv_sem):
    me = lax.axis_index("res")
    stages = bits_of(n)
    greet(me, stages)
    base = [n - (n >> s) for s in range(stages)]

    def copy(s, h):
        rel = (2 * h + 1) << s
        slot = base[s] + h
        return pltpu.make_async_remote_copy(
            src_ref=x_ref.at[peer(me, rel)] if s == 0 else acc.at[rel // 2],
            dst_ref=recv.at[slot],
            send_sem=send_sem.at[slot],
            recv_sem=recv_sem.at[slot],
            device_id={"res": peer(me, 1 << s)},
            device_id_type=MESH,
        )

    def order(s):
        names = range(n >> (s + 1))
        return sorted(names, key=lambda h: ((h & -h) or n, -h))

    copies = {}
    for h in order(0):
        copies[0, h] = copy(0, h)
        copies[0, h].start()
    rows = x_ref.shape[1]
    part = min(rows, 128)
    for s in range(stages):
        for h in order(s):
            copies[s, h].wait_recv()
            rel = h << (s + 1)
            slot = base[s] + h
            source = x_ref.at[peer(me, rel)] if s == 0 else acc.at[rel // 2]

            @pl.loop(0, rows // part)
            def _(r):
                at = pl.ds(pl.multiple_of(r * part, part), part)
                total = source[at].astype(jnp.float32) + recv[slot, at].astype(jnp.float32)
                if s == stages - 1:
                    out_ref[at] = total
                else:
                    acc[rel // 2, at] = total.astype(jnp.bfloat16)

            if h % 2 == 1:
                copies[s + 1, h // 2] = copy(s + 1, h // 2)
                copies[s + 1, h // 2].start()
    for each in copies.values():
        each.wait_send()


def reduce_scatter(blocks):
    n, rows, width = blocks.shape
    return pl.pallas_call(
        functools.partial(scatter_kernel, n),
        out_shape=jax.ShapeDtypeStruct((rows, width), jnp.float32),
        in_specs=[pl.BlockSpec(memory_space=pltpu.VMEM)],
        out_specs=pl.BlockSpec(memory_space=pltpu.VMEM),
        scratch_shapes=[
            pltpu.VMEM((n // 2, rows, width), jnp.bfloat16),
            pltpu.VMEM((n - 1, rows, width), jnp.bfloat16),
            pltpu.SemaphoreType.DMA((n - 1,)),
            pltpu.SemaphoreType.DMA((n - 1,)),
        ],
        compiler_params=pltpu.CompilerParams(
            collective_id=0, has_side_effects=True, vmem_limit_bytes=VMEM_LIMIT
        ),
        name="reduce_scatter",
    )(blocks)


def gather_kernel(n, x_ref, out_ref, send_sem, recv_sem):
    me = lax.axis_index("res")
    stages = bits_of(n)
    greet(me, stages)
    base = [n - (n >> s) for s in range(stages)]

    def copy(s, h):
        owner = peer(me, h << (s + 1))
        slot = base[s] + h
        return pltpu.make_async_remote_copy(
            src_ref=x_ref if h == 0 else out_ref.at[owner],
            dst_ref=out_ref.at[owner],
            send_sem=send_sem.at[slot],
            recv_sem=recv_sem.at[slot],
            device_id={"res": peer(me, 1 << s)},
            device_id_type=MESH,
        )

    copies = {}

    def pass_on(rel, stage):
        for s in reversed(range(stage)):
            copies[s, rel >> (s + 1)] = copy(s, rel >> (s + 1))
            copies[s, rel >> (s + 1)].start()

    pass_on(0, stages)
    out_ref[me] = x_ref[...]
    waits = [(s, h) for s in range(stages) for h in range(n >> (s + 1))]
    hops = lambda s, h: bin((2 * h + 1) << s).count("1")
    waits.sort(key=lambda sh: (hops(*sh) - stages, sh) if sh[0] >= 2 else (stages - sh[0], sh))
    for s, h in waits:
        copies[s, h].wait_recv()
        pass_on((2 * h + 1) << s, s)
    for each in copies.values():
        each.wait_send()


def all_gather(block, n):
    rows, width = block.shape
    return pl.pallas_call(
        functools.partial(gather_kernel, n),
        out_shape=jax.ShapeDtypeStruct((n, rows, width), block.dtype),
        in_specs=[pl.BlockSpec(memory_space=pltpu.VMEM)],
        out_specs=pl.BlockSpec(memory_space=pltpu.VMEM),
        scratch_shapes=[
            pltpu.SemaphoreType.DMA((n - 1,)),
            pltpu.SemaphoreType.DMA((n - 1,)),
        ],
        compiler_params=pltpu.CompilerParams(
            collective_id=1, has_side_effects=True, vmem_limit_bytes=VMEM_LIMIT
        ),
        name="all_gather",
    )(block)


def masked(shape, first, rows_ref, tile_ref, chain_ref):
    count = shape[0] // chain_ref.shape[0]
    parts = [(chain_ref[...] == rows_ref[0, first + m]) | (tile_ref[...] > 0) for m in range(count)]
    return parts[0] if count == 1 else jnp.concatenate(parts, axis=0)


def normed_parts(pair, gain, bias):
    values = pair.astype(jnp.float32)
    center = jnp.mean(values, axis=-1, keepdims=True)
    values = values - center
    scale = lax.rsqrt(jnp.mean(values * values, axis=-1, keepdims=True) + 1e-05)
    unit = values * scale
    return unit, scale, (unit * gain + bias).astype(jnp.bfloat16)


def gated(normed, both_ref):
    hidden = both_ref.shape[1] // 2
    products = jnp.dot(normed, both_ref[...], preferred_element_type=jnp.float32)
    return products[:, :hidden], 0.5 * jnp.tanh(0.5 * products[:, hidden:]) + 0.5


def forward_kernel(rows_ref, pair_ref, gain_ref, bias_ref, both_ref, tile_ref, chain_ref, out_ref):
    inner = chain_ref.shape[0]
    step = max(inner, min(256, pair_ref.shape[0]))
    ratio = step // inner
    start = pl.program_id(0) * (pair_ref.shape[0] // inner)

    @pl.loop(0, pair_ref.shape[0] // step)
    def _(t):
        at = pl.ds(pl.multiple_of(t * step, step), step)
        unused, unused, normed = normed_parts(pair_ref[at], gain_ref[...], bias_ref[...])
        value, gating = gated(normed, both_ref)
        keep = masked((step,), start + t * ratio, rows_ref, tile_ref, chain_ref)
        out_ref[at] = jnp.where(keep, gating * value, 0.0).astype(jnp.bfloat16)


def backward_kernel(
    rows_ref, pair_ref, grad_ref, gain_ref, bias_ref, both_ref, back_ref, tile_ref, chain_ref, out_ref
):
    inner = chain_ref.shape[0]
    step = max(inner, min(256, pair_ref.shape[0]))
    ratio = step // inner
    start = pl.program_id(0) * (pair_ref.shape[0] // inner)

    @pl.loop(0, pair_ref.shape[0] // step)
    def _(t):
        at = pl.ds(pl.multiple_of(t * step, step), step)
        gain = gain_ref[...]
        unit, scale, normed = normed_parts(pair_ref[at], gain, bias_ref[...])
        value, gating = gated(normed, both_ref)
        keep = masked((step,), start + t * ratio, rows_ref, tile_ref, chain_ref)
        grad = jnp.where(keep, grad_ref[at].astype(jnp.float32), 0.0)
        grad_value = grad * gating
        grad_gate = grad_value * value * (1.0 - gating)
        pulled = jnp.concatenate(
            [grad_value.astype(jnp.bfloat16), grad_gate.astype(jnp.bfloat16)], axis=1
        )
        grad_normed = jnp.dot(pulled, back_ref[...], preferred_element_type=jnp.float32)
        grad_unit = grad_normed.astype(jnp.bfloat16).astype(jnp.float32) * gain
        mean_grad = jnp.mean(grad_unit, axis=-1, keepdims=True)
        mean_dot = jnp.mean(grad_unit * unit, axis=-1, keepdims=True)
        out_ref[at] = (scale * (grad_unit - mean_grad - unit * mean_dot)).astype(jnp.bfloat16)


def per_row(kernel, name, streamed, fixed, chain_rows, inner, width):
    rows = streamed[0].shape[0]
    block = min(rows, 2048)
    whole = lambda array: pl.BlockSpec(array.shape, lambda g: (0, 0))
    return pl.pallas_call(
        kernel,
        grid=(rows // block,),
        out_shape=jax.ShapeDtypeStruct((rows, width), jnp.bfloat16),
        in_specs=[pl.BlockSpec(memory_space=pltpu.SMEM)]
        + [pl.BlockSpec((block, each.shape[1]), lambda g: (g, 0)) for each in streamed]
        + [whole(each) for each in fixed],
        out_specs=pl.BlockSpec((block, width), lambda g: (g, 0)),
        compiler_params=pltpu.CompilerParams(vmem_limit_bytes=VMEM_LIMIT),
        name=name,
    )(chain_rows[None, :], *streamed, *fixed)


def layer_norm(values, gain, bias):
    values = values.astype(jnp.float32)
    center = jnp.mean(values, axis=-1, keepdims=True)
    spread = jnp.mean(jnp.square(values - center), axis=-1, keepdims=True)
    return (values - center) * lax.rsqrt(spread + 1e-05) * gain + bias


def output_gate(tri, pair, norm_gain, norm_bias, tri_gain, tri_bias, weight_out, gate_out):
    normed = layer_norm(pair, norm_gain, norm_bias).astype(jnp.bfloat16)
    gating = jax.nn.sigmoid(jnp.dot(normed, gate_out, preferred_element_type=jnp.float32))
    scaled = layer_norm(tri, tri_gain, tri_bias).astype(jnp.bfloat16)
    return gating * jnp.dot(scaled, weight_out, preferred_element_type=jnp.float32)


def local(
    pair_left,
    pair_right,
    pair_block,
    grad_out,
    norm_gain,
    norm_bias,
    weight_left,
    gate_left,
    weight_right,
    gate_right,
    tri_gain,
    tri_bias,
    weight_out,
    gate_out,
    tile_left,
    tile_right,
    chain_rows,
    chain_slab,
    chain_cols,
):
    slab_rows = pair_left.shape[1]
    block_cols = pair_block.shape[0]
    tile_rows = slab_rows // tile_left.shape[1]
    row_total, unused, channels = pair_left.shape
    col_total = pair_right.shape[1]
    hidden = weight_left.shape[1]
    gain, bias = norm_gain[None, :], norm_bias[None, :]
    spread = lambda line: jnp.broadcast_to(line[:, None], (line.shape[0], hidden))
    tiles_left = spread(jnp.repeat(tile_left[0], tile_rows))
    tiles_right = spread(jnp.repeat(tile_right[0], block_cols))
    chains_left, chains_right = spread(chain_slab), spread(chain_cols)
    both_left = jnp.concatenate([weight_left, gate_left], axis=1)
    both_right = jnp.concatenate([weight_right, gate_right], axis=1)
    rows_left = pair_left.reshape(row_total * slab_rows, channels)
    rows_right = pair_right.reshape(row_total * col_total, channels)
    left = per_row(
        forward_kernel, "left_forward", [rows_left],
        [gain, bias, both_left, tiles_left, chains_left], chain_rows, slab_rows, hidden,
    ).reshape(row_total, slab_rows, hidden)
    right = per_row(
        forward_kernel, "right_forward", [rows_right],
        [gain, bias, both_right, tiles_right, chains_right], chain_rows, col_total, hidden,
    ).reshape(row_total, col_total, hidden)
    axis_size = col_total // block_cols
    share = jnp.einsum("kic,kjc->jic", left, right, preferred_element_type=jnp.float32)
    tri = reduce_scatter(
        share.astype(jnp.bfloat16).reshape(axis_size, block_cols * slab_rows, hidden)
    ).reshape(block_cols, slab_rows, hidden)
    result, out_back = jax.vjp(
        lambda product, pair: output_gate(
            product, pair, norm_gain, norm_bias, tri_gain, tri_bias, weight_out, gate_out
        ),
        tri,
        pair_block,
    )
    grad_tri, block_grad = out_back(grad_out.astype(jnp.float32))
    sent = grad_tri.astype(jnp.bfloat16)

    gathered = all_gather(sent.reshape(block_cols * slab_rows, hidden), axis_size)
    gathered = gathered.reshape(col_total, slab_rows, hidden)
    total_left = jnp.einsum("jic,kjc->kic", gathered, right, preferred_element_type=jnp.float32)
    total_right = jnp.einsum("kic,jic->kjc", left, gathered, preferred_element_type=jnp.float32)
    grad_left = per_row(
        backward_kernel, "left_backward",
        [rows_left, total_left.astype(jnp.bfloat16).reshape(row_total * slab_rows, hidden)],
        [gain, bias, both_left, both_left.T, tiles_left, chains_left],
        chain_rows, slab_rows, channels,
    ).reshape(pair_left.shape)
    grad_right = per_row(
        backward_kernel, "right_backward",
        [rows_right, total_right.astype(jnp.bfloat16).reshape(row_total * col_total, hidden)],
        [gain, bias, both_right, both_right.T, tiles_right, chains_right],
        chain_rows, col_total, channels,
    ).reshape(pair_right.shape)
    return (grad_left, grad_right, block_grad)


def solution(mesh):
    placed = (
        P(("groups", "res"), None, None),
        P(("groups", "res"), None, None),
        P(("groups", "res"), None, None),
        P(("groups", "res"), None, None),
        P(),
        P(),
        P(),
        P(),
        P(),
        P(),
        P(),
        P(),
        P(),
        P(),
        P(("groups", "res"), None),
        P(("groups", "res"), None),
        P(("groups", "res")),
        P("groups"),
        P("groups"),
    )
    return jax.shard_map(
        local,
        mesh=mesh,
        in_specs=placed,
        out_specs=(
            P(("groups", "res"), None, None),
            P(("groups", "res"), None, None),
            P(("groups", "res"), None, None),
        ),
        check_vma=False,
    )
```

```python
import functools

import jax
import jax.numpy as jnp
from jax import lax
from jax.experimental import pallas as pl
from jax.experimental.pallas import tpu as pltpu
from jax.sharding import PartitionSpec as P


MESH = pl.DeviceIdType.MESH
VMEM_LIMIT = 48 * 1024 * 1024
UNROLL = 1


def bits_of(count):
    return count.bit_length() - 1


def peer(me, rel):
    other = me
    for s in range(rel.bit_length()):
        if (rel >> s) & 1:
            step = 1 << s
            other = other + step * (1 - 2 * lax.rem(lax.div(me, step), 2))
    return other


def greet(me, stages):
    barrier = pltpu.get_barrier_semaphore()
    for s in range(stages):
        pl.semaphore_signal(
            barrier, inc=1, device_id={"res": peer(me, 1 << s)}, device_id_type=MESH
        )
    pl.semaphore_wait(barrier, stages)


def scatter_kernel(n, x_ref, out_ref, acc, recv, send_sem, recv_sem):
    me = lax.axis_index("res")
    stages = bits_of(n)
    greet(me, stages)
    base = [n - (n >> s) for s in range(stages)]

    def copy(s, h):
        rel = (2 * h + 1) << s
        slot = base[s] + h
        return pltpu.make_async_remote_copy(
            src_ref=x_ref.at[peer(me, rel)] if s == 0 else acc.at[rel // 2],
            dst_ref=recv.at[slot],
            send_sem=send_sem.at[slot],
            recv_sem=recv_sem.at[slot],
            device_id={"res": peer(me, 1 << s)},
            device_id_type=MESH,
        )

    def order(s):
        names = range(n >> (s + 1))
        return sorted(names, key=lambda h: ((h & -h) or n, -h))

    copies = {}
    for h in order(0):
        copies[0, h] = copy(0, h)
        copies[0, h].start()
    rows = x_ref.shape[1]
    part = min(rows, 128)
    for s in range(stages):
        for h in order(s):
            copies[s, h].wait_recv()
            rel = h << (s + 1)
            slot = base[s] + h
            source = x_ref.at[peer(me, rel)] if s == 0 else acc.at[rel // 2]

            @pl.loop(0, rows // part)
            def _(r):
                at = pl.ds(pl.multiple_of(r * part, part), part)
                total = source[at].astype(jnp.float32) + recv[slot, at].astype(jnp.float32)
                if s == stages - 1:
                    out_ref[at] = total
                else:
                    acc[rel // 2, at] = total.astype(jnp.bfloat16)

            if h % 2 == 1:
                copies[s + 1, h // 2] = copy(s + 1, h // 2)
                copies[s + 1, h // 2].start()
    for each in copies.values():
        each.wait_send()


def reduce_scatter(blocks):
    n, rows, width = blocks.shape
    return pl.pallas_call(
        functools.partial(scatter_kernel, n),
        out_shape=jax.ShapeDtypeStruct((rows, width), jnp.float32),
        in_specs=[pl.BlockSpec(memory_space=pltpu.VMEM)],
        out_specs=pl.BlockSpec(memory_space=pltpu.VMEM),
        scratch_shapes=[
            pltpu.VMEM((n // 2, rows, width), jnp.bfloat16),
            pltpu.VMEM((n - 1, rows, width), jnp.bfloat16),
            pltpu.SemaphoreType.DMA((n - 1,)),
            pltpu.SemaphoreType.DMA((n - 1,)),
        ],
        compiler_params=pltpu.CompilerParams(
            collective_id=0, has_side_effects=True, vmem_limit_bytes=VMEM_LIMIT
        ),
        name="reduce_scatter",
    )(blocks)


def gather_kernel(n, x_ref, out_ref, send_sem, recv_sem):
    me = lax.axis_index("res")
    stages = bits_of(n)
    greet(me, stages)
    base = [n - (n >> s) for s in range(stages)]

    def copy(s, h):
        owner = peer(me, h << (s + 1))
        slot = base[s] + h
        return pltpu.make_async_remote_copy(
            src_ref=x_ref if h == 0 else out_ref.at[owner],
            dst_ref=out_ref.at[owner],
            send_sem=send_sem.at[slot],
            recv_sem=recv_sem.at[slot],
            device_id={"res": peer(me, 1 << s)},
            device_id_type=MESH,
        )

    copies = {}

    def pass_on(rel, stage):
        for s in reversed(range(stage)):
            copies[s, rel >> (s + 1)] = copy(s, rel >> (s + 1))
            copies[s, rel >> (s + 1)].start()

    pass_on(0, stages)
    out_ref[me] = x_ref[...]
    waits = [(s, h) for s in range(stages) for h in range(n >> (s + 1))]
    hops = lambda s, h: bin((2 * h + 1) << s).count("1")
    waits.sort(key=lambda sh: (hops(*sh) - stages, sh) if sh[0] >= 2 else (stages - sh[0], sh))
    for s, h in waits:
        copies[s, h].wait_recv()
        pass_on((2 * h + 1) << s, s)
    for each in copies.values():
        each.wait_send()


def all_gather(block, n):
    rows, width = block.shape
    return pl.pallas_call(
        functools.partial(gather_kernel, n),
        out_shape=jax.ShapeDtypeStruct((n, rows, width), block.dtype),
        in_specs=[pl.BlockSpec(memory_space=pltpu.VMEM)],
        out_specs=pl.BlockSpec(memory_space=pltpu.VMEM),
        scratch_shapes=[
            pltpu.SemaphoreType.DMA((n - 1,)),
            pltpu.SemaphoreType.DMA((n - 1,)),
        ],
        compiler_params=pltpu.CompilerParams(
            collective_id=1, has_side_effects=True, vmem_limit_bytes=VMEM_LIMIT
        ),
        name="all_gather",
    )(block)


def masked(shape, first, rows_ref, tile_ref, chain_ref):
    count = shape[0] // chain_ref.shape[0]
    parts = [(chain_ref[...] == rows_ref[0, first + m]) | (tile_ref[...] > 0) for m in range(count)]
    return parts[0] if count == 1 else jnp.concatenate(parts, axis=0)


def row_means(values):
    width = values.shape[-1]
    share = jnp.full((width, width), 1.0 / width, jnp.bfloat16)
    return jnp.dot(values.astype(jnp.bfloat16), share, preferred_element_type=jnp.float32)


def normed_parts(pair, gain, bias):
    values = pair.astype(jnp.float32) - row_means(pair)
    scale = lax.rsqrt(row_means(values * values) + 1e-05)
    unit = values * scale
    return unit, scale, (unit * gain + bias).astype(jnp.bfloat16)


def gated(normed, both_ref):
    hidden = both_ref.shape[1] // 2
    products = jnp.dot(normed, both_ref[...], preferred_element_type=jnp.float32)
    return products[:, :hidden], 0.5 * jnp.tanh(0.5 * products[:, hidden:]) + 0.5


def forward_kernel(rows_ref, pair_ref, gain_ref, bias_ref, both_ref, tile_ref, chain_ref, out_ref):
    inner = chain_ref.shape[0]
    step = max(inner, min(2048, pair_ref.shape[0]))
    ratio = step // inner
    start = pl.program_id(0) * (pair_ref.shape[0] // inner)

    @pl.loop(0, pair_ref.shape[0] // step, unroll=UNROLL)
    def _(t):
        at = pl.ds(pl.multiple_of(t * step, step), step)
        unused, unused, normed = normed_parts(pair_ref[at], gain_ref[...], bias_ref[...])
        value, gating = gated(normed, both_ref)
        keep = masked((step,), start + t * ratio, rows_ref, tile_ref, chain_ref)
        out_ref[at] = jnp.where(keep, gating * value, 0.0).astype(jnp.bfloat16)


def backward_kernel(
    rows_ref, pair_ref, grad_ref, gain_ref, bias_ref, both_ref, back_ref, tile_ref, chain_ref, out_ref
):
    inner = chain_ref.shape[0]
    step = max(inner, min(2048, pair_ref.shape[0]))
    ratio = step // inner
    start = pl.program_id(0) * (pair_ref.shape[0] // inner)

    @pl.loop(0, pair_ref.shape[0] // step, unroll=UNROLL)
    def _(t):
        at = pl.ds(pl.multiple_of(t * step, step), step)
        gain = gain_ref[...]
        unit, scale, normed = normed_parts(pair_ref[at], gain, bias_ref[...])
        value, gating = gated(normed, both_ref)
        keep = masked((step,), start + t * ratio, rows_ref, tile_ref, chain_ref)
        grad = jnp.where(keep, grad_ref[at].astype(jnp.float32), 0.0)
        grad_value = grad * gating
        grad_gate = grad_value * value * (1.0 - gating)
        pulled = jnp.concatenate(
            [grad_value.astype(jnp.bfloat16), grad_gate.astype(jnp.bfloat16)], axis=1
        )
        grad_normed = jnp.dot(pulled, back_ref[...], preferred_element_type=jnp.float32)
        grad_unit = grad_normed.astype(jnp.bfloat16).astype(jnp.float32) * gain
        mean_grad = row_means(grad_unit)
        mean_dot = row_means(grad_unit * unit)
        out_ref[at] = (scale * (grad_unit - mean_grad - unit * mean_dot)).astype(jnp.bfloat16)


def per_row(kernel, name, streamed, fixed, chain_rows, inner, width):
    rows = streamed[0].shape[0]
    block = min(rows, 4096)
    whole = lambda array: pl.BlockSpec(array.shape, lambda g: (0, 0))
    return pl.pallas_call(
        kernel,
        grid=(rows // block,),
        out_shape=jax.ShapeDtypeStruct((rows, width), jnp.bfloat16),
        in_specs=[pl.BlockSpec(memory_space=pltpu.SMEM)]
        + [pl.BlockSpec((block, each.shape[1]), lambda g: (g, 0)) for each in streamed]
        + [whole(each) for each in fixed],
        out_specs=pl.BlockSpec((block, width), lambda g: (g, 0)),
        compiler_params=pltpu.CompilerParams(vmem_limit_bytes=VMEM_LIMIT),
        name=name,
    )(chain_rows[None, :], *streamed, *fixed)


def layer_norm(values, gain, bias):
    values = values.astype(jnp.float32)
    center = jnp.mean(values, axis=-1, keepdims=True)
    spread = jnp.mean(jnp.square(values - center), axis=-1, keepdims=True)
    return (values - center) * lax.rsqrt(spread + 1e-05) * gain + bias


def output_gate(tri, pair, norm_gain, norm_bias, tri_gain, tri_bias, weight_out, gate_out):
    normed = layer_norm(pair, norm_gain, norm_bias).astype(jnp.bfloat16)
    gating = jax.nn.sigmoid(jnp.dot(normed, gate_out, preferred_element_type=jnp.float32))
    scaled = layer_norm(tri, tri_gain, tri_bias).astype(jnp.bfloat16)
    return gating * jnp.dot(scaled, weight_out, preferred_element_type=jnp.float32)


def local(
    pair_left,
    pair_right,
    pair_block,
    grad_out,
    norm_gain,
    norm_bias,
    weight_left,
    gate_left,
    weight_right,
    gate_right,
    tri_gain,
    tri_bias,
    weight_out,
    gate_out,
    tile_left,
    tile_right,
    chain_rows,
    chain_slab,
    chain_cols,
):
    slab_rows = pair_left.shape[1]
    block_cols = pair_block.shape[0]
    tile_rows = slab_rows // tile_left.shape[1]
    row_total, unused, channels = pair_left.shape
    col_total = pair_right.shape[1]
    hidden = weight_left.shape[1]
    gain, bias = norm_gain[None, :], norm_bias[None, :]
    spread = lambda line: jnp.broadcast_to(line[:, None], (line.shape[0], hidden))
    tiles_left = spread(jnp.repeat(tile_left[0], tile_rows))
    tiles_right = spread(jnp.repeat(tile_right[0], block_cols))
    chains_left, chains_right = spread(chain_slab), spread(chain_cols)
    both_left = jnp.concatenate([weight_left, gate_left], axis=1)
    both_right = jnp.concatenate([weight_right, gate_right], axis=1)
    rows_left = pair_left.reshape(row_total * slab_rows, channels)
    rows_right = pair_right.reshape(row_total * col_total, channels)
    left = per_row(
        forward_kernel, "left_forward", [rows_left],
        [gain, bias, both_left, tiles_left, chains_left], chain_rows, slab_rows, hidden,
    ).reshape(row_total, slab_rows, hidden)
    right = per_row(
        forward_kernel, "right_forward", [rows_right],
        [gain, bias, both_right, tiles_right, chains_right], chain_rows, col_total, hidden,
    ).reshape(row_total, col_total, hidden)
    axis_size = col_total // block_cols
    share = jnp.einsum("kic,kjc->jic", left, right, preferred_element_type=jnp.float32)
    tri = reduce_scatter(
        share.astype(jnp.bfloat16).reshape(axis_size, block_cols * slab_rows, hidden)
    ).reshape(block_cols, slab_rows, hidden)
    result, out_back = jax.vjp(
        lambda product, pair: output_gate(
            product, pair, norm_gain, norm_bias, tri_gain, tri_bias, weight_out, gate_out
        ),
        tri,
        pair_block,
    )
    grad_tri, block_grad = out_back(grad_out.astype(jnp.float32))
    sent = grad_tri.astype(jnp.bfloat16)

    gathered = all_gather(sent.reshape(block_cols * slab_rows, hidden), axis_size)
    gathered = gathered.reshape(col_total, slab_rows, hidden)
    total_left = jnp.einsum("jic,kjc->kic", gathered, right, preferred_element_type=jnp.float32)
    total_right = jnp.einsum("kic,jic->kjc", left, gathered, preferred_element_type=jnp.float32)
    grad_left = per_row(
        backward_kernel, "left_backward",
        [rows_left, total_left.astype(jnp.bfloat16).reshape(row_total * slab_rows, hidden)],
        [gain, bias, both_left, both_left.T, tiles_left, chains_left],
        chain_rows, slab_rows, channels,
    ).reshape(pair_left.shape)
    grad_right = per_row(
        backward_kernel, "right_backward",
        [rows_right, total_right.astype(jnp.bfloat16).reshape(row_total * col_total, hidden)],
        [gain, bias, both_right, both_right.T, tiles_right, chains_right],
        chain_rows, col_total, channels,
    ).reshape(pair_right.shape)
    return (grad_left, grad_right, block_grad)


def solution(mesh):
    placed = (
        P(("groups", "res"), None, None),
        P(("groups", "res"), None, None),
        P(("groups", "res"), None, None),
        P(("groups", "res"), None, None),
        P(),
        P(),
        P(),
        P(),
        P(),
        P(),
        P(),
        P(),
        P(),
        P(),
        P(("groups", "res"), None),
        P(("groups", "res"), None),
        P(("groups", "res")),
        P("groups"),
        P("groups"),
    )
    return jax.shard_map(
        local,
        mesh=mesh,
        in_specs=placed,
        out_specs=(
            P(("groups", "res"), None, None),
            P(("groups", "res"), None, None),
            P(("groups", "res"), None, None),
        ),
        check_vma=False,
    )
```

```python
import functools

import jax
import jax.numpy as jnp
from jax import lax
from jax.experimental import pallas as pl
from jax.experimental.pallas import tpu as pltpu
from jax.sharding import PartitionSpec as P


MESH = pl.DeviceIdType.MESH
VMEM_LIMIT = 48 * 1024 * 1024
UNROLL = 1


def bits_of(count):
    return count.bit_length() - 1


def peer(me, rel):
    other = me
    for s in range(rel.bit_length()):
        if (rel >> s) & 1:
            step = 1 << s
            other = other + step * (1 - 2 * lax.rem(lax.div(me, step), 2))
    return other


def greet(me, stages):
    barrier = pltpu.get_barrier_semaphore()
    for s in range(stages):
        pl.semaphore_signal(
            barrier, inc=1, device_id={"res": peer(me, 1 << s)}, device_id_type=MESH
        )
    pl.semaphore_wait(barrier, stages)


def scatter_kernel(n, x_ref, out_ref, acc, recv, send_sem, recv_sem):
    me = lax.axis_index("res")
    stages = bits_of(n)
    greet(me, stages)
    base = [n - (n >> s) for s in range(stages)]

    def copy(s, h):
        rel = (2 * h + 1) << s
        slot = base[s] + h
        return pltpu.make_async_remote_copy(
            src_ref=x_ref.at[peer(me, rel)] if s == 0 else acc.at[rel // 2],
            dst_ref=recv.at[slot],
            send_sem=send_sem.at[slot],
            recv_sem=recv_sem.at[slot],
            device_id={"res": peer(me, 1 << s)},
            device_id_type=MESH,
        )

    def order(s):
        names = range(n >> (s + 1))
        return sorted(names, key=lambda h: ((h & -h) or n, -h))

    copies = {}
    for h in order(0):
        copies[0, h] = copy(0, h)
        copies[0, h].start()
    rows = x_ref.shape[1]
    part = min(rows, 1024)
    for s in range(stages):
        for h in order(s):
            copies[s, h].wait_recv()
            rel = h << (s + 1)
            slot = base[s] + h
            source = x_ref.at[peer(me, rel)] if s == 0 else acc.at[rel // 2]

            @pl.loop(0, rows // part)
            def _(r):
                at = pl.ds(pl.multiple_of(r * part, part), part)
                total = source[at].astype(jnp.float32) + recv[slot, at].astype(jnp.float32)
                if s == stages - 1:
                    out_ref[at] = total
                else:
                    acc[rel // 2, at] = total.astype(jnp.bfloat16)

            if h % 2 == 1:
                copies[s + 1, h // 2] = copy(s + 1, h // 2)
                copies[s + 1, h // 2].start()
    for each in copies.values():
        each.wait_send()


def reduce_scatter(blocks):
    n, rows, width = blocks.shape
    return pl.pallas_call(
        functools.partial(scatter_kernel, n),
        out_shape=jax.ShapeDtypeStruct((rows, width), jnp.float32),
        in_specs=[pl.BlockSpec(memory_space=pltpu.VMEM)],
        out_specs=pl.BlockSpec(memory_space=pltpu.VMEM),
        scratch_shapes=[
            pltpu.VMEM((n // 2, rows, width), jnp.bfloat16),
            pltpu.VMEM((n - 1, rows, width), jnp.bfloat16),
            pltpu.SemaphoreType.DMA((n - 1,)),
            pltpu.SemaphoreType.DMA((n - 1,)),
        ],
        compiler_params=pltpu.CompilerParams(
            collective_id=0, has_side_effects=True, vmem_limit_bytes=VMEM_LIMIT
        ),
        name="reduce_scatter",
    )(blocks)


def gather_kernel(n, x_ref, out_ref, send_sem, recv_sem):
    me = lax.axis_index("res")
    stages = bits_of(n)
    greet(me, stages)
    base = [n - (n >> s) for s in range(stages)]

    def copy(s, h):
        owner = peer(me, h << (s + 1))
        slot = base[s] + h
        return pltpu.make_async_remote_copy(
            src_ref=x_ref if h == 0 else out_ref.at[owner],
            dst_ref=out_ref.at[owner],
            send_sem=send_sem.at[slot],
            recv_sem=recv_sem.at[slot],
            device_id={"res": peer(me, 1 << s)},
            device_id_type=MESH,
        )

    copies = {}

    def pass_on(rel, stage):
        for s in reversed(range(stage)):
            copies[s, rel >> (s + 1)] = copy(s, rel >> (s + 1))
            copies[s, rel >> (s + 1)].start()

    pass_on(0, stages)
    out_ref[me] = x_ref[...]
    waits = [(s, h) for s in range(stages) for h in range(n >> (s + 1))]
    hops = lambda s, h: bin((2 * h + 1) << s).count("1")
    waits.sort(key=lambda sh: (hops(*sh) - stages, sh) if sh[0] >= 2 else (stages - sh[0], sh))
    for s, h in waits:
        copies[s, h].wait_recv()
        pass_on((2 * h + 1) << s, s)
    for each in copies.values():
        each.wait_send()


def all_gather(block, n):
    rows, width = block.shape
    return pl.pallas_call(
        functools.partial(gather_kernel, n),
        out_shape=jax.ShapeDtypeStruct((n, rows, width), block.dtype),
        in_specs=[pl.BlockSpec(memory_space=pltpu.VMEM)],
        out_specs=pl.BlockSpec(memory_space=pltpu.VMEM),
        scratch_shapes=[
            pltpu.SemaphoreType.DMA((n - 1,)),
            pltpu.SemaphoreType.DMA((n - 1,)),
        ],
        compiler_params=pltpu.CompilerParams(
            collective_id=1, has_side_effects=True, vmem_limit_bytes=VMEM_LIMIT
        ),
        name="all_gather",
    )(block)


def masked(shape, first, rows_ref, tile_ref, chain_ref):
    count = shape[0] // chain_ref.shape[0]
    parts = [(chain_ref[...] == rows_ref[0, first + m]) | (tile_ref[...] > 0) for m in range(count)]
    return parts[0] if count == 1 else jnp.concatenate(parts, axis=0)


def row_means(values):
    width = values.shape[-1]
    share = jnp.full((width, width), 1.0 / width, jnp.bfloat16)
    return jnp.dot(values.astype(jnp.bfloat16), share, preferred_element_type=jnp.float32)


def normed_parts(pair, gain, bias):
    values = pair.astype(jnp.float32) - row_means(pair)
    scale = lax.rsqrt(row_means(values * values) + 1e-05)
    unit = values * scale
    return unit, scale, (unit * gain + bias).astype(jnp.bfloat16)


def gated(normed, both_ref):
    hidden = both_ref.shape[1] // 2
    products = jnp.dot(normed, both_ref[...], preferred_element_type=jnp.float32)
    return products[:, :hidden], 0.5 * jnp.tanh(0.5 * products[:, hidden:]) + 0.5


def forward_kernel(rows_ref, pair_ref, gain_ref, bias_ref, both_ref, tile_ref, chain_ref, out_ref):
    inner = chain_ref.shape[0]
    step = max(inner, min(2048, pair_ref.shape[0]))
    ratio = step // inner
    start = pl.program_id(0) * (pair_ref.shape[0] // inner)

    @pl.loop(0, pair_ref.shape[0] // step, unroll=UNROLL)
    def _(t):
        at = pl.ds(pl.multiple_of(t * step, step), step)
        unused, unused, normed = normed_parts(pair_ref[at], gain_ref[...], bias_ref[...])
        value, gating = gated(normed, both_ref)
        keep = masked((step,), start + t * ratio, rows_ref, tile_ref, chain_ref)
        out_ref[at] = jnp.where(keep, gating * value, 0.0).astype(jnp.bfloat16)


def backward_kernel(
    rows_ref, pair_ref, grad_ref, gain_ref, bias_ref, both_ref, tile_ref, chain_ref, out_ref
):
    inner = chain_ref.shape[0]
    step = max(inner, min(2048, pair_ref.shape[0]))
    ratio = step // inner
    start = pl.program_id(0) * (pair_ref.shape[0] // inner)

    @pl.loop(0, pair_ref.shape[0] // step, unroll=UNROLL)
    def _(t):
        at = pl.ds(pl.multiple_of(t * step, step), step)
        gain = gain_ref[...]
        unit, scale, normed = normed_parts(pair_ref[at], gain, bias_ref[...])
        value, gating = gated(normed, both_ref)
        keep = masked((step,), start + t * ratio, rows_ref, tile_ref, chain_ref)
        grad = jnp.where(keep, grad_ref[at].astype(jnp.float32), 0.0)
        grad_value = grad * gating
        grad_gate = grad_value * value * (1.0 - gating)
        pulled = jnp.concatenate(
            [grad_value.astype(jnp.bfloat16), grad_gate.astype(jnp.bfloat16)], axis=1
        )
        grad_normed = lax.dot_general(
            pulled, both_ref[...], (((1,), (1,)), ((), ())), preferred_element_type=jnp.float32
        )
        grad_unit = grad_normed.astype(jnp.bfloat16).astype(jnp.float32) * gain
        mean_grad = row_means(grad_unit)
        mean_dot = row_means(grad_unit * unit)
        out_ref[at] = (scale * (grad_unit - mean_grad - unit * mean_dot)).astype(jnp.bfloat16)


def per_row(kernel, name, streamed, fixed, chain_rows, inner, width):
    rows = streamed[0].shape[0]
    block = min(rows, 4096)
    whole = lambda array: pl.BlockSpec(array.shape, lambda g: (0, 0))
    return pl.pallas_call(
        kernel,
        grid=(rows // block,),
        out_shape=jax.ShapeDtypeStruct((rows, width), jnp.bfloat16),
        in_specs=[pl.BlockSpec(memory_space=pltpu.SMEM)]
        + [pl.BlockSpec((block, each.shape[1]), lambda g: (g, 0)) for each in streamed]
        + [whole(each) for each in fixed],
        out_specs=pl.BlockSpec((block, width), lambda g: (g, 0)),
        compiler_params=pltpu.CompilerParams(vmem_limit_bytes=VMEM_LIMIT),
        name=name,
    )(chain_rows[None, :], *streamed, *fixed)


def layer_norm(values, gain, bias):
    values = values.astype(jnp.float32)
    center = jnp.mean(values, axis=-1, keepdims=True)
    spread = jnp.mean(jnp.square(values - center), axis=-1, keepdims=True)
    return (values - center) * lax.rsqrt(spread + 1e-05) * gain + bias


def output_gate(tri, pair, norm_gain, norm_bias, tri_gain, tri_bias, weight_out, gate_out):
    normed = layer_norm(pair, norm_gain, norm_bias).astype(jnp.bfloat16)
    gating = jax.nn.sigmoid(jnp.dot(normed, gate_out, preferred_element_type=jnp.float32))
    scaled = layer_norm(tri, tri_gain, tri_bias).astype(jnp.bfloat16)
    return gating * jnp.dot(scaled, weight_out, preferred_element_type=jnp.float32)


def local(
    pair_left,
    pair_right,
    pair_block,
    grad_out,
    norm_gain,
    norm_bias,
    weight_left,
    gate_left,
    weight_right,
    gate_right,
    tri_gain,
    tri_bias,
    weight_out,
    gate_out,
    tile_left,
    tile_right,
    chain_rows,
    chain_slab,
    chain_cols,
):
    slab_rows = pair_left.shape[1]
    block_cols = pair_block.shape[0]
    tile_rows = slab_rows // tile_left.shape[1]
    row_total, unused, channels = pair_left.shape
    col_total = pair_right.shape[1]
    hidden = weight_left.shape[1]
    gain, bias = norm_gain[None, :], norm_bias[None, :]
    spread = lambda line: jnp.broadcast_to(line[:, None], (line.shape[0], hidden))
    tiles_left = spread(jnp.repeat(tile_left[0], tile_rows))
    tiles_right = spread(jnp.repeat(tile_right[0], block_cols))
    chains_left, chains_right = spread(chain_slab), spread(chain_cols)
    both_left = jnp.concatenate([weight_left, gate_left], axis=1)
    both_right = jnp.concatenate([weight_right, gate_right], axis=1)
    rows_left = pair_left.reshape(row_total * slab_rows, channels)
    rows_right = pair_right.reshape(row_total * col_total, channels)
    left = per_row(
        forward_kernel, "left_forward", [rows_left],
        [gain, bias, both_left, tiles_left, chains_left], chain_rows, slab_rows, hidden,
    ).reshape(row_total, slab_rows, hidden)
    right = per_row(
        forward_kernel, "right_forward", [rows_right],
        [gain, bias, both_right, tiles_right, chains_right], chain_rows, col_total, hidden,
    ).reshape(row_total, col_total, hidden)
    axis_size = col_total // block_cols
    share = jnp.einsum("kic,kjc->jic", left, right, preferred_element_type=jnp.float32)
    tri = reduce_scatter(
        share.astype(jnp.bfloat16).reshape(axis_size, block_cols * slab_rows, hidden)
    ).reshape(block_cols, slab_rows, hidden)
    result, out_back = jax.vjp(
        lambda product, pair: output_gate(
            product, pair, norm_gain, norm_bias, tri_gain, tri_bias, weight_out, gate_out
        ),
        tri,
        pair_block,
    )
    grad_tri, block_grad = out_back(grad_out.astype(jnp.float32))
    sent = grad_tri.astype(jnp.bfloat16)

    gathered = all_gather(sent.reshape(block_cols * slab_rows, hidden), axis_size)
    gathered = gathered.reshape(col_total, slab_rows, hidden)
    total_left = jnp.einsum("jic,kjc->kic", gathered, right, preferred_element_type=jnp.float32)
    total_right = jnp.einsum("kic,jic->kjc", left, gathered, preferred_element_type=jnp.float32)
    grad_left = per_row(
        backward_kernel, "left_backward",
        [rows_left, total_left.astype(jnp.bfloat16).reshape(row_total * slab_rows, hidden)],
        [gain, bias, both_left, tiles_left, chains_left],
        chain_rows, slab_rows, channels,
    ).reshape(pair_left.shape)
    grad_right = per_row(
        backward_kernel, "right_backward",
        [rows_right, total_right.astype(jnp.bfloat16).reshape(row_total * col_total, hidden)],
        [gain, bias, both_right, tiles_right, chains_right],
        chain_rows, col_total, channels,
    ).reshape(pair_right.shape)
    return (grad_left, grad_right, block_grad)


def solution(mesh):
    placed = (
        P(("groups", "res"), None, None),
        P(("groups", "res"), None, None),
        P(("groups", "res"), None, None),
        P(("groups", "res"), None, None),
        P(),
        P(),
        P(),
        P(),
        P(),
        P(),
        P(),
        P(),
        P(),
        P(),
        P(("groups", "res"), None),
        P(("groups", "res"), None),
        P(("groups", "res")),
        P("groups"),
        P("groups"),
    )
    return jax.shard_map(
        local,
        mesh=mesh,
        in_specs=placed,
        out_specs=(
            P(("groups", "res"), None, None),
            P(("groups", "res"), None, None),
            P(("groups", "res"), None, None),
        ),
        check_vma=False,
    )
```
